512 devices in a mesh: row: 16 (over y_hi, x, core), col: 32 (over y_lo, z).
Axes of the slice: x: 4, y: 8 (y_hi: 2, y_lo: 4; y = y_hi * 4 + y_lo), z: 8, core: 2. Of those that a mesh axis runs over, the one named last changes fastest.
Arguments:
- density: bfloat16 [2, 12288, 12288], P(None, 'row', 'col'), may hold values from -6 to 6
- hcols: int32 [96, 4], P('row'), may hold values from -1 to 95, as said below
- hvals: bfloat16 [96, 4, 128, 128], P('row'), may hold values from -0.25 to 0.25
Outputs:
- propagated: float32 [2, 12288, 12288], P(None, 'row', 'col')
The draws below stay inside these ranges and needn't reach their ends.
Inputs may be any that keep to these rules, and one draw needn't show every extreme that they name: In block row b the first slots of hcols hold b and then, in increasing order, some of b + 1 to b + 3, all below 96; the remaining slots hold -1.
All inputs are finite; a program needn't handle non-finite values.
Results may differ from the reference program's by a relative error of at most 0.0022.
Values may be sent and summed in bfloat16 or wider, within the bound.
No kernel may reach another device: no remote copies, remote signals or barrier semaphores. Data moves between devices by JAX's collectives and lax.ppermute only.
A program may use at most 128 MiB of HBM per device.

```python
import jax
import jax.numpy as jnp
from jax import lax

BLK = 128
BAND = 3
KSLOT = 4
NB = 96
N = 12288


def draw_hcols(key, part):
    key = jax.random.fold_in(key, 7)
    region_key, pick_key = jax.random.split(key)
    regions = (NB + 7) // 8
    level = jax.random.randint(region_key, (regions,), 1, 9)
    row_level = jnp.repeat(level, 8)[:NB]
    rolls = jax.random.randint(pick_key, (NB, BAND), 0, 8)
    rows = jnp.arange(NB, dtype=jnp.int32)
    offsets = jnp.arange(1, BAND + 1, dtype=jnp.int32)
    present = (rolls < row_level[:, None]) & (rows[:, None] + offsets[None, :] < NB)
    marks = jnp.concatenate([jnp.ones((NB, 1), jnp.int32), present.astype(jnp.int32)], axis=1)
    position = jnp.cumsum(marks, axis=1) - 1
    columns = rows[:, None] + jnp.arange(BAND + 1, dtype=jnp.int32)[None, :]
    slots = jnp.arange(BAND + 1, dtype=jnp.int32)
    hit = (marks[:, :, None] == 1) & (position[:, :, None] == slots[None, None, :])
    value = jnp.sum(jnp.where(hit, columns[:, :, None], 0), axis=1)
    filled = jnp.sum(marks, axis=1)
    return jnp.where(slots[None, :] < filled[:, None], value, -1).astype(jnp.int32)


def block_scale(stream_key, dims, cuts, smallest, high):
    gain = 1.0
    for dim, shards_of in cuts:
        steps = jax.random.uniform(jax.random.fold_in(jax.random.fold_in(stream_key, 6), dim), (shards_of,), jnp.float32, smallest / len(cuts), high / len(cuts))
        gain = gain * jnp.repeat(jnp.exp(steps), dims[dim] // shards_of).reshape((-1,) + (1,) * (len(dims) - 1 - dim))
    return gain


def bell_draw(own_key, shape, scale, most, cuts=(), kind=jnp.bfloat16):
    drawn = jax.random.normal(own_key, shape, jnp.float32) * scale
    if len(cuts) > 0:
        drawn = block_scale(own_key, shape, cuts, -0.22, 0.18) * drawn
    return jnp.clip(drawn, min=-most, max=most).astype(kind)


def setup_inputs(seed: int = 0) -> dict:
    splits = jax.random.split(jax.random.key(seed), 4)
    density = bell_draw(splits[0], (2, N, N), 1.0, 6.0, ((1, 16), (2, 32)))
    hcols = draw_hcols(jax.random.fold_in(splits[3], 71), 0)
    hvals = bell_draw(splits[2], (NB, KSLOT, BLK, BLK), (4 * BLK) ** -0.5, 0.25, ((0, 16),))
    return {"density": density, "hcols": hcols, "hvals": hvals}


DT = 0.5


def band_blocks(upper, lower):
    count = upper.shape[0]
    ext = jnp.concatenate([lower, upper], axis=0)
    pieces = []
    for q in range(2 * BAND + 1):
        offset = q - BAND
        if offset > 0:
            pieces.append(ext[BAND:, offset])
        elif offset < 0:
            pieces.append(jnp.swapaxes(ext[BAND + offset:BAND + offset + count, -offset], 1, 2))
        else:
            diag = ext[BAND:, 0].astype(jnp.float32)
            pieces.append((diag + jnp.swapaxes(diag, 1, 2)).astype(jnp.bfloat16))
    return jnp.stack(pieces, axis=1)


def reference(density, hcols, hvals):
    rows = jnp.arange(NB, dtype=jnp.int32)
    targets = rows[:, None] + jnp.arange(BAND + 1, dtype=jnp.int32)[None, :]
    onehot = (hcols[:, None, :] == targets[:, :, None]).astype(jnp.float32)
    upper = jnp.einsum('bps,bsxy->bpxy', onehot, hvals.astype(jnp.float32)).astype(jnp.bfloat16)
    lower = jnp.zeros((BAND, BAND + 1, BLK, BLK), jnp.bfloat16)
    band = band_blocks(upper, lower)
    wide = (2 * BAND + 1) * BLK
    hrow = band.transpose(0, 2, 1, 3).reshape(NB, BLK, wide)
    bandf = band.astype(jnp.float32)
    margin = BAND * BLK

    def rate(padded, b):
        start = (b * BLK).astype(jnp.int32)
        slab = lax.dynamic_slice(padded, (jnp.int32(0), start, jnp.int32(margin)), (2, wide, N))
        hline = lax.dynamic_index_in_dim(hrow, b, 0, keepdims=False)
        left = jnp.stack([jnp.dot(hline, slab[0], preferred_element_type=jnp.float32),
                          jnp.dot(hline, slab[1], preferred_element_type=jnp.float32)])
        stripe = lax.dynamic_slice(padded, (jnp.int32(0), start + margin, jnp.int32(0)),
                                   (2, BLK, N + 2 * margin)).astype(jnp.float32)
        right = jnp.zeros((2, BLK, NB, BLK), jnp.float32)
        for q in range(2 * BAND + 1):
            window = stripe[:, :, q * BLK:q * BLK + N].reshape(2, BLK, NB, BLK)
            right = right + jnp.einsum('pijy,jxy->pijx', window, bandf[:, q])
        comm = left - right.reshape(2, BLK, N)
        return jnp.stack([comm[1], -comm[0]])

    def own_rows(b):
        start = (b * BLK).astype(jnp.int32)
        return lax.dynamic_slice(density, (jnp.int32(0), start, jnp.int32(0)), (2, BLK, N)).astype(jnp.float32)

    pad_first = jnp.pad(density, ((0, 0), (margin, margin), (margin, margin)))

    def first_section(b):
        first_rate = rate(pad_first, b)
        return (own_rows(b) + DT * first_rate).astype(jnp.bfloat16), first_rate

    middle, first_rates = lax.map(first_section, rows)
    middle = middle.transpose(1, 0, 2, 3).reshape(2, N, N)
    pad_second = jnp.pad(middle, ((0, 0), (margin, margin), (margin, margin)))

    def second_section(items):
        b, first_rate = items
        second_rate = rate(pad_second, b)
        return own_rows(b) + (DT / 2) * (first_rate + second_rate)

    result = lax.map(second_section, (rows, first_rates))
    return result.transpose(1, 0, 2, 3).reshape(2, N, N)
```

```python
import jax
import jax.numpy as jnp
from jax import lax
from jax.experimental import pallas as pl
from jax.experimental.pallas import tpu as pltpu
from jax.sharding import PartitionSpec as P

BLK = 128
BAND = 3
DT = 0.5

Y_HI, X, CORE = 2, 4, 2
Y_LO, Z = 4, 8
ROWS = Y_HI * X * CORE
COLS = Y_LO * Z
TALL = 6 * BLK
WIDE = 3 * BLK
MARGIN = BAND * BLK
PAIR = 2 * BLK
HALF = TALL // 2

CROSSING = [(r, p) for r in range(-BAND, 0) for p in range(1, BAND + 1) if r + p >= 0]

F32 = jnp.float32
BF16 = jnp.bfloat16
MIB = 1 << 20
VMEM = pl.BlockSpec(memory_space=pltpu.VMEM)


def params(mib):
    return pltpu.CompilerParams(vmem_limit_bytes=mib * MIB)


def cost(flops, bytes_accessed):
    return pl.CostEstimate(flops=flops, bytes_accessed=bytes_accessed, transcendentals=0)


def to_column(block, distance):
    return lax.ppermute(block, "col", [(i - distance, i) for i in range(COLS) if 0 <= i - distance < COLS])


OWN_CHIPS = [
    16267594, 12429704, 9998170, 9706963, 16353610, 16038288, 10063690, 9809793, 10538199, 10538654, 15231692,
    13466180, 10538143, 10615892, 13421191, 12103196, 16300816, 15773016, 12074762, 11571098, 4109616,
    12428080, 3343851, 3343851, 11616129, 9801617, 16324931, 9973579, 16095632, 16300368, 9707418, 9969498,
]
CROSSING_CHIPS = [
    13973960, 10067778, 16259411, 9805712, 14432586, 9015153, 13998530, 12934852, 12701521, 14736596, 15551557,
    14805588, 11325062, 10776220, 11030110, 2258165, 4142376, 11580912, 4107544, 11541971, 4109616, 13713217,
    9995755, 9969498, 5345193, 16258347, 15741866, 16259411, 9748368, 9805712, 9969498,
]


def routes(kind, chips):
    pairs = []
    for tile in range(ROWS):
        for col in range(COLS):
            y_lo, z = divmod(col, Z)
            away = (z - 2 * tile + 1 - kind) % Z
            target = 2 * tile + away // 2 + kind
            if away < 4 and target < COLS:
                chip = chips[2 * tile + away // 2] >> 3 * (away % 2 * Y_LO + y_lo) & 7
                pairs.append((tile * COLS + col, (chip * CORE + kind) * COLS + target))
    return pairs


def core_index():
    return lax.rem(lax.axis_index("row"), CORE)


def start_kernel(hcols, hvals, top, bottom, upper, own, crossing, to_chip, to_core):
    tile = lax.axis_index("row")
    z = lax.rem(lax.axis_index("col"), Z)
    for i in range(6):
        b = tile * 6 + i
        upper[4 * i] = hvals[i, 0]
        for p in range(1, BAND + 1):
            block = jnp.zeros((BLK, BLK), BF16)
            for s in range(1, p + 1):
                block = jnp.where(hcols[i, s] == b + p, hvals[i, s], block)
            upper[4 * i + p] = block
    away = lax.rem(z - 2 * tile + 1 + 2 * ROWS, Z)
    half = lax.rem(away // 2, 2)
    own[...] = upper[pl.ds(half * 12, 12)]
    away = lax.rem(z - 2 * tile + 2 * ROWS, Z)
    half = lax.rem(away // 2, 2)
    for k, (r, p) in enumerate(CROSSING):
        crossing[k] = upper[half * 12 + 4 * (r + 3) + p]

    def fill(above, below):
        for part in range(2):
            for k in range(3):
                rows = slice(k * BLK, (k + 1) * BLK)
                above[3 * part + k] = top[part, rows]
                below[3 * part + k] = bottom[part, rows]
        for k, (r, p) in enumerate(CROSSING):
            below[6 + k // 3, :, k % 3 * BLK : (k % 3 + 1) * BLK] = upper[4 * (r + 6) + p]

    core = core_index()

    @pl.when(core == 0)
    def _():
        fill(to_chip, to_core)

    @pl.when(core == 1)
    def _():
        fill(to_core, to_chip)


def both(block):
    wide = block.astype(F32)
    return (wide + wide.T).astype(BF16)


def right_band_kernel(halves, across, band):
    core = core_index()

    def own(k):
        return jnp.where(core == 0, halves[k], across[k])

    def crossing(k):
        return jnp.where(core == 0, across[k], halves[k])

    for r in range(9):
        for j in range(3):
            offset = j + BAND - r
            if abs(offset) > BAND:
                block = jnp.zeros((BLK, BLK), BF16)
            elif offset > 0 and r < BAND:
                block = crossing(CROSSING.index((r - BAND, offset)))
            elif offset > 0:
                block = own(4 * (r - BAND) + offset)
            elif offset == 0:
                block = both(own(4 * j))
            else:
                block = own(4 * j - offset).T
            band[r * BLK : (r + 1) * BLK, j * BLK : (j + 1) * BLK] = block


def left_products(band, ext, pair):
    return jnp.dot(band[pair], ext[pair * PAIR : pair * PAIR + 1024, :], preferred_element_type=F32)


def first_left_kernel(field, from_chip, from_core, upper, out, band, ext):
    core = core_index()
    for part in range(2):
        at = slice(part * WIDE, (part + 1) * WIDE)
        for k in range(3):
            one, two = from_chip[3 * part + k], from_core[3 * part + k]
            ext[k * BLK : (k + 1) * BLK, at] = jnp.where(core == 0, one, two)
            ext[MARGIN + TALL + k * BLK : MARGIN + TALL + (k + 1) * BLK, at] = jnp.where(core == 0, two, one)
        ext[MARGIN : MARGIN + TALL, at] = field[part]

    def low(k):
        at = slice(k % 3 * BLK, (k % 3 + 1) * BLK)
        return jnp.where(core == 0, from_chip[6 + k // 3, :, at], from_core[6 + k // 3, :, at])

    for pair in range(3):
        for i in range(2):
            b = 2 * pair + i
            for c in range(8):
                offset = c - BAND - i
                if abs(offset) > BAND:
                    block = jnp.zeros((BLK, BLK), BF16)
                elif offset > 0:
                    block = upper[4 * b + offset]
                elif offset == 0:
                    block = both(upper[4 * b])
                elif b + offset >= 0:
                    block = upper[4 * (b + offset) - offset].T
                else:
                    block = low(CROSSING.index((b + offset, -offset))).T
                band[pair, i * BLK : (i + 1) * BLK, c * BLK : (c + 1) * BLK] = block
    for pair in range(3):
        product = left_products(band, ext, pair)
        rows = slice(pair * PAIR, (pair + 1) * PAIR)
        out[0, rows] = product[:, :WIDE]
        out[1, rows] = product[:, WIDE:]


def first_right_kernel(before, field, after, other, left, band, middle, total, to_chip, to_core):
    stretch = jnp.concatenate([before[0], field[0], after[0]], axis=1)
    product = jnp.concatenate(
        [
            jnp.dot(stretch[:, :1024], band[:1024, :256], preferred_element_type=F32),
            jnp.dot(stretch[:, 256:], band[256:, 256:], preferred_element_type=F32),
        ],
        axis=1,
    )
    sign = jnp.where(pl.program_id(0) == 0, -1.0, 1.0)
    rate = sign * (left[0] - product)
    start = other[0].astype(F32)
    stepped = (start + DT * rate).astype(BF16)
    middle[0] = stepped
    total[0] = start + (DT / 2) * rate

    outward = pl.program_id(1) == core_index()

    @pl.when(outward)
    def _():
        to_chip[0] = stepped

    @pl.when(jnp.logical_not(outward))
    def _():
        to_core[0] = stepped


def second_left_kernel(middle, from_chip, from_core, band, right_band, total, out, ext):
    core = core_index()
    for part in range(2):
        at = slice(part * WIDE, (part + 1) * WIDE)
        one, two = from_chip[part], from_core[part]
        ext[:MARGIN, at] = jnp.where(core == 0, one, two)
        ext[MARGIN : MARGIN + TALL, at] = middle[part]
        ext[MARGIN + TALL :, at] = jnp.where(core == 0, two, one)
    centre = right_band[MARGIN : MARGIN + WIDE, :]
    for pair in range(3):
        rows = slice(pair * PAIR, (pair + 1) * PAIR)
        product = left_products(band, ext, pair)
        own_re = jnp.dot(middle[0, rows], centre, preferred_element_type=F32)
        own_im = jnp.dot(middle[1, rows], centre, preferred_element_type=F32)
        out[0, rows] = total[0, rows] + (DT / 2) * (product[:, WIDE:] - own_im)
        out[1, rows] = total[1, rows] - (DT / 2) * (product[:, :WIDE] - own_re)


def last_kernel(before, after, total, band, out):
    product = jnp.dot(before[0], band[:MARGIN, :], preferred_element_type=F32)
    product = product + jnp.dot(after[0], band[MARGIN + WIDE :, :], preferred_element_type=F32)
    sign = jnp.where(pl.program_id(0) == 0, 1.0, -1.0)
    out[0] = total[0] + (sign * DT / 2) * product


SAME = pl.BlockSpec((1, HALF, WIDE), lambda p, h: (p, h, 0))
OTHER = pl.BlockSpec((1, HALF, WIDE), lambda p, h: (1 - p, h, 0))
OTHER_EDGE = pl.BlockSpec((1, HALF, WIDE), lambda p, h: (1 - p, 0, 0))
BANDS = pl.BlockSpec((9 * BLK, WIDE), lambda p, h: (0, 0))


def to_other_core(block):
    return lax.ppermute(block, "row", [(i, i ^ 1) for i in range(ROWS)])


def to_other_chip(block):
    ends = [(i, i + 1) for i in range(1, ROWS - 1, 2)]
    return lax.ppermute(block, "row", ends + [(j, i) for i, j in ends])


def on_device(density, hcols, hvals):
    before = to_column(density, 1)
    after = to_column(density, -1)
    top = pl.BlockSpec((2, MARGIN, WIDE), lambda _: (0, 0, 0))
    bottom = pl.BlockSpec((2, MARGIN, WIDE), lambda _: (0, 1, 0))
    upper, own, crossing, to_chip, to_core = pl.pallas_call(
        start_kernel,
        grid=(1,),
        in_specs=[pl.BlockSpec(memory_space=pltpu.SMEM), VMEM, top, bottom],
        out_specs=[VMEM] * 5,
        out_shape=[
            jax.ShapeDtypeStruct((24, BLK, BLK), BF16),
            jax.ShapeDtypeStruct((12, BLK, BLK), BF16),
            jax.ShapeDtypeStruct((6, BLK, BLK), BF16),
            jax.ShapeDtypeStruct((8, BLK, WIDE), BF16),
            jax.ShapeDtypeStruct((8, BLK, WIDE), BF16),
        ],
        compiler_params=params(56),
        cost_estimate=cost(0, 4 * MIB),
        name="start",
    )(hcols, hvals, density, density)
    own = lax.ppermute(own, ("row", "col"), routes(0, OWN_CHIPS))
    crossing = lax.ppermute(crossing, ("row", "col"), routes(1, CROSSING_CHIPS))
    halves = jnp.where(core_index() == 0, own, jnp.concatenate([crossing, crossing], axis=0))
    across = to_other_core(halves)
    from_chip = to_other_chip(to_chip)
    from_core = to_other_core(to_core)
    left, left_band = pl.pallas_call(
        first_left_kernel,
        in_specs=[VMEM] * 4,
        out_specs=[VMEM] * 2,
        out_shape=[
            jax.ShapeDtypeStruct((2, TALL, WIDE), F32),
            jax.ShapeDtypeStruct((3, PAIR, 1024), BF16),
        ],
        scratch_shapes=[pltpu.VMEM((TALL + 2 * MARGIN, 2 * WIDE), BF16)],
        compiler_params=params(24),
        cost_estimate=cost(2 * TALL * 1024 * 2 * WIDE, 8 * MIB),
        name="first_left",
    )(density, from_chip, from_core, upper)
    right_band = pl.pallas_call(
        right_band_kernel,
        in_specs=[VMEM] * 2,
        out_specs=VMEM,
        out_shape=jax.ShapeDtypeStruct((9 * BLK, WIDE), BF16),
        compiler_params=params(16),
        cost_estimate=cost(0, 2 * MIB),
        name="right_band",
    )(halves, across)
    middle, total, to_chip, to_core = pl.pallas_call(
        first_right_kernel,
        grid=(2, 2),
        in_specs=[SAME, SAME, SAME, OTHER, SAME, BANDS],
        out_specs=[OTHER, OTHER, OTHER_EDGE, OTHER_EDGE],
        out_shape=[
            jax.ShapeDtypeStruct((2, TALL, WIDE), BF16),
            jax.ShapeDtypeStruct((2, TALL, WIDE), F32),
            jax.ShapeDtypeStruct((2, MARGIN, WIDE), BF16),
            jax.ShapeDtypeStruct((2, MARGIN, WIDE), BF16),
        ],
        compiler_params=params(24),
        cost_estimate=cost(4 * TALL * 9 * BLK * WIDE, 14 * MIB),
        name="first_right",
    )(before, density, after, density, left, right_band)

    before = to_column(middle, 1)
    after = to_column(middle, -1)
    from_chip = to_other_chip(to_chip)
    from_core = to_other_core(to_core)
    total = pl.pallas_call(
        second_left_kernel,
        in_specs=[VMEM] * 6,
        out_specs=VMEM,
        out_shape=jax.ShapeDtypeStruct((2, TALL, WIDE), F32),
        scratch_shapes=[pltpu.VMEM((TALL + 2 * MARGIN, 2 * WIDE), BF16)],
        compiler_params=params(32),
        cost_estimate=cost(2 * TALL * 1408 * 2 * WIDE, 10 * MIB),
        name="second_left",
    )(middle, from_chip, from_core, left_band, right_band, total)
    return pl.pallas_call(
        last_kernel,
        grid=(2, 2),
        in_specs=[SAME, SAME, OTHER, BANDS],
        out_specs=OTHER,
        out_shape=jax.ShapeDtypeStruct((2, TALL, WIDE), F32),
        compiler_params=params(24),
        cost_estimate=cost(4 * TALL * 6 * BLK * WIDE, 8 * MIB),
        name="last",
    )(before, after, total, right_band)


def solution(mesh):
    placed = (P(None, "row", "col"), P("row", None), P("row", None, None, None))
    return jax.shard_map(
        on_device, mesh=mesh, in_specs=placed, out_specs=P(None, "row", "col"), check_vma=False
    )
```

```python
import functools

import jax
import jax.numpy as jnp
from jax import lax
from jax.experimental import pallas as pl
from jax.experimental.pallas import tpu as pltpu
from jax.sharding import PartitionSpec as P

BLK = 128
BAND = 3
DT = 0.5

Y_HI, X, CORE = 2, 4, 2
Y_LO, Z = 4, 8
ROWS = Y_HI * X * CORE
COLS = Y_LO * Z
TALL = 6 * BLK
WIDE = 3 * BLK
MARGIN = BAND * BLK
PAIR = 2 * BLK
HALF = TALL // 2

CROSSING = [(r, p) for r in range(-BAND, 0) for p in range(1, BAND + 1) if r + p >= 0]

F32 = jnp.float32
BF16 = jnp.bfloat16
MIB = 1 << 20
VMEM = pl.BlockSpec(memory_space=pltpu.VMEM)


def params(mib):
    return pltpu.CompilerParams(vmem_limit_bytes=mib * MIB)


def cost(flops, bytes_accessed):
    return pl.CostEstimate(flops=flops, bytes_accessed=bytes_accessed, transcendentals=0)


def to_column(block, distance):
    return lax.ppermute(block, "col", [(i - distance, i) for i in range(COLS) if 0 <= i - distance < COLS])


OWN_CHIPS = [
    0o57234610, 0o65324710, 0o47106532, 0o46217530, 0o75104623, 0o65314720, 0o47205631, 0o46107523, 0o41356207,
    0o61354207, 0o72046135, 0o42067135, 0o71354206, 0o41357206, 0o72064135, 0o76024135, 0o37516402, 0o17502463,
    0o24631750, 0o14602753, 0o37521460, 0o7632451, 0o14523760, 0o2735461, 0o64027513, 0o54217603, 0o76035421,
    0o75206413, 0o46137520, 0o75234601, 0o76015423, 0o65137420,
]
CROSSING_CHIPS = [
    0o46207531, 0o45107623, 0o67124530, 0o45126730, 0o65104732, 0o47325610, 0o57304612, 0o71045236, 0o50264731,
    0o60145732, 0o57324016, 0o62345017, 0o50176324, 0o72165034, 0o50246713, 0o23645017, 0o34721560, 0o54723601,
    0o36510472, 0o14520673, 0o56732401, 0o46032571, 0o17532640, 0o75136402, 0o45107623, 0o76034512, 0o46017523,
    0o76235401, 0o75106423, 0o56017423, 0o76235410,
]


def routes(kind, chips):
    pairs = []
    for tile in range(ROWS):
        for col in range(COLS):
            y_lo, z = divmod(col, Z)
            away = (z - 2 * tile + 1 - kind) % Z
            target = 2 * tile + away // 2 + kind
            if away < 4 and target < COLS:
                chip = chips[2 * tile + away // 2] >> 3 * (away % 2 * Y_LO + y_lo) & 7
                pairs.append((tile * COLS + col, (chip * CORE + kind) * COLS + target))
    return pairs


def core_index():
    return lax.rem(lax.axis_index("row"), CORE)


def start_kernel(hcols, hvals, upper, own, crossing, low):
    tile = lax.axis_index("row")
    z = lax.rem(lax.axis_index("col"), Z)
    for i in range(6):
        b = tile * 6 + i
        upper[4 * i] = hvals[i, 0]
        for p in range(1, BAND + 1):
            block = jnp.zeros((BLK, BLK), BF16)
            for s in range(1, p + 1):
                named = jnp.broadcast_to(hcols[s : s + 1, i : i + 1] == b + p, (BLK, BLK))
                block = jnp.where(named, hvals[i, s], block)
            upper[4 * i + p] = block
    away = lax.rem(z - 2 * tile + 1 + 2 * ROWS, Z)
    half = lax.rem(away // 2, 2)
    own[...] = upper[pl.ds(half * 12, 12)]
    away = lax.rem(z - 2 * tile + 2 * ROWS, Z)
    half = lax.rem(away // 2, 2)
    for k, (r, p) in enumerate(CROSSING):
        crossing[k] = upper[half * 12 + 4 * (r + 3) + p]
        low[k // 3 * BLK : (k // 3 + 1) * BLK, k % 3 * BLK : (k % 3 + 1) * BLK] = upper[4 * (r + 6) + p]


def edge(density, low, row):
    rows = lax.dynamic_slice_in_dim(density, row, MARGIN, 1)
    return jnp.concatenate([rows.reshape(2 * MARGIN, WIDE), low], axis=0)


def both(block):
    wide = block.astype(F32)
    return (wide + wide.T).astype(BF16)


def right_band_kernel(halves, across, band):
    core = core_index()

    def own(k):
        return jnp.where(core == 0, halves[k], across[k])

    def crossing(k):
        return jnp.where(core == 0, across[k], halves[k])

    for r in range(9):
        for j in range(3):
            offset = j + BAND - r
            if abs(offset) > BAND:
                block = jnp.zeros((BLK, BLK), BF16)
            elif offset > 0 and r < BAND:
                block = crossing(CROSSING.index((r - BAND, offset)))
            elif offset > 0:
                block = own(4 * (r - BAND) + offset)
            elif offset == 0:
                block = both(own(4 * j))
            else:
                block = own(4 * j - offset).T
            band[r * BLK : (r + 1) * BLK, j * BLK : (j + 1) * BLK] = block


def inner_products(band, field, pair):
    first, stop = max(0, pair * PAIR - MARGIN), min(TALL, pair * PAIR + PAIR + MARGIN)
    columns = slice(first - pair * PAIR + MARGIN, stop - pair * PAIR + MARGIN)
    both_parts = jnp.concatenate([field[0, first:stop], field[1, first:stop]], axis=1)
    return jnp.dot(band[pair][:, columns], both_parts, preferred_element_type=F32)


def first_left_kernel(field, upper, out, band, below_band):
    for pair in range(3):
        for i in range(2):
            b = 2 * pair + i
            for c in range(8):
                offset = c - BAND - i
                if abs(offset) > BAND or b + offset < 0:
                    block = jnp.zeros((BLK, BLK), BF16)
                elif offset > 0:
                    block = upper[4 * b + offset]
                elif offset == 0:
                    block = both(upper[4 * b])
                else:
                    block = upper[4 * (b + offset) - offset].T
                band[pair, i * BLK : (i + 1) * BLK, c * BLK : (c + 1) * BLK] = block
    for i in range(3):
        for c in range(3):
            block = upper[4 * (3 + i) + 3 + c - i] if c <= i else jnp.zeros((BLK, BLK), BF16)
            below_band[i * BLK : (i + 1) * BLK, c * BLK : (c + 1) * BLK] = block
    for pair in range(3):
        product = inner_products(band, field, pair)
        rows = slice(pair * PAIR, (pair + 1) * PAIR)
        out[0, rows] = product[:, :WIDE]
        out[1, rows] = product[:, WIDE:]


def first_right_kernel(
    before, field, after, left, band, chip_far, core_far, below_band,
    middle, total, to_chip, to_core, above_band, from_chip, from_core, sems,
):
    core = core_index()
    copies = [
        pltpu.make_async_copy(far, near, sems.at[k])
        for k, (far, near) in enumerate(((chip_far, from_chip), (core_far, from_core)))
    ]
    for copy in copies:
        copy.start()
    for part in range(2):
        for k in range(2):
            rows = slice(k * MARGIN, (k + 1) * MARGIN)
            stretch = jnp.concatenate([before[part, rows], field[part, rows], after[part, rows]], axis=1)
            product = jnp.concatenate(
                [
                    jnp.dot(stretch[:, :1024], band[:1024, :256], preferred_element_type=F32),
                    jnp.dot(stretch[:, 256:], band[256:, 256:], preferred_element_type=F32),
                ],
                axis=1,
            )
            total[1 - part, rows] = left[part, rows] - product
    for copy in copies:
        copy.wait()
    for i in range(3):
        for c in range(3):
            block = jnp.zeros((BLK, BLK), BF16)
            if c >= i:
                k = CROSSING.index((c - 3, i + 3 - c))
                rows = slice(2 * MARGIN + k // 3 * BLK, 2 * MARGIN + (k // 3 + 1) * BLK)
                at = slice(k % 3 * BLK, (k % 3 + 1) * BLK)
                block = jnp.where(core == 0, from_chip[rows, at], from_core[rows, at]).T
            above_band[i * BLK : (i + 1) * BLK, c * BLK : (c + 1) * BLK] = block
    for part in range(2):
        other, sign = 1 - part, (-1.0, 1.0)[part]
        one, two = (side[part * MARGIN : (part + 1) * MARGIN] for side in (from_chip, from_core))
        halves = (
            (above_band, jnp.where(core == 0, one, two)),
            (below_band, jnp.where(core == 0, two, one)),
        )
        for k, (outer, beyond) in enumerate(halves):
            rows = slice(k * MARGIN, (k + 1) * MARGIN)
            far = jnp.dot(outer[...], beyond, preferred_element_type=F32)
            rate = sign * (total[other, rows] + far)
            start = field[other, rows].astype(F32)
            middle[other, rows] = (start + DT * rate).astype(BF16)
            total[other, rows] = start + (DT / 2) * rate
        to_chip[other] = middle[other, pl.ds(pl.multiple_of(core * MARGIN, MARGIN), MARGIN)]
        to_core[other] = middle[other, pl.ds(pl.multiple_of((1 - core) * MARGIN, MARGIN), MARGIN)]


def second_left_kernel(middle, band, right_band, total, out):
    centre = right_band[MARGIN : MARGIN + WIDE, :]
    for pair in range(3):
        rows = slice(pair * PAIR, (pair + 1) * PAIR)
        product = inner_products(band, middle, pair)
        own_re = jnp.dot(middle[0, rows], centre, preferred_element_type=F32)
        own_im = jnp.dot(middle[1, rows], centre, preferred_element_type=F32)
        out[0, rows] = total[0, rows] + (DT / 2) * (product[:, WIDE:] - own_im)
        out[1, rows] = total[1, rows] - (DT / 2) * (product[:, :WIDE] - own_re)


def last_kernel(before, after, total, band, from_chip, from_core, above_band, below_band, out, result, sems):
    core = core_index()
    copies = []
    for part in range(2):
        other, sign = 1 - part, (-1.0, 1.0)[part]
        halves = (
            (above_band, jnp.where(core == 0, from_chip[part], from_core[part])),
            (below_band, jnp.where(core == 0, from_core[part], from_chip[part])),
        )
        for k, (outer, beyond) in enumerate(halves):
            rows = slice(k * MARGIN, (k + 1) * MARGIN)
            product = jnp.dot(before[part, rows], band[:MARGIN, :], preferred_element_type=F32)
            product = product + jnp.dot(after[part, rows], band[MARGIN + WIDE :, :], preferred_element_type=F32)
            far = jnp.dot(outer[...], beyond, preferred_element_type=F32)
            result[other, rows] = total[other, rows] + (sign * DT / 2) * (far - product)
            at = pl.ds(k * MARGIN, MARGIN)
            copies.append(pltpu.make_async_copy(result.at[other, at], out.at[other, at], sems.at[2 * part + k]))
            copies[-1].start()
    for copy in copies:
        copy.wait()


def to_other_core(block):
    return lax.ppermute(block, "row", [(i, i ^ 1) for i in range(ROWS)])


def to_other_chip(block):
    ends = [(i, i + 1) for i in range(1, ROWS - 1, 2)]
    return lax.ppermute(block, "row", ends + [(j, i) for i, j in ends])


def on_device(density, hcols, hvals):
    before = to_column(density, 1)
    after = to_column(density, -1)
    any_space = pl.BlockSpec(memory_space=pl.ANY)
    upper, own, crossing, low = pl.pallas_call(
        start_kernel,
        in_specs=[VMEM] * 2,
        out_specs=[VMEM] * 4,
        out_shape=[
            jax.ShapeDtypeStruct((24, BLK, BLK), BF16),
            jax.ShapeDtypeStruct((12, BLK, BLK), BF16),
            jax.ShapeDtypeStruct((6, BLK, BLK), BF16),
            jax.ShapeDtypeStruct((2 * BLK, WIDE), BF16),
        ],
        compiler_params=params(56),
        cost_estimate=cost(0, 2 * MIB),
        name="start",
    )(hcols.T, hvals)
    to_chip = edge(density, low, core_index() * MARGIN)
    to_core = edge(density, low, (1 - core_index()) * MARGIN)
    own = lax.ppermute(own, ("row", "col"), routes(0, OWN_CHIPS))
    crossing = lax.ppermute(crossing, ("row", "col"), routes(1, CROSSING_CHIPS))
    left, left_band, below_band = pl.pallas_call(
        first_left_kernel,
        in_specs=[VMEM] * 2,
        out_specs=[VMEM] * 3,
        out_shape=[
            jax.ShapeDtypeStruct((2, TALL, WIDE), F32),
            jax.ShapeDtypeStruct((3, PAIR, 1024), BF16),
            jax.ShapeDtypeStruct((MARGIN, MARGIN), BF16),
        ],
        compiler_params=params(20),
        cost_estimate=cost(2 * TALL * 1024 * 2 * WIDE, 8 * MIB),
        name="first_left",
    )(density, upper)
    own, _ = lax.optimization_barrier((own, left_band))
    halves = jnp.where(core_index() == 0, own, jnp.concatenate([crossing, crossing], axis=0))
    across = to_other_core(halves)
    to_core, _ = lax.optimization_barrier((to_core, crossing))
    from_chip = to_other_chip(to_chip)
    from_core = to_other_core(to_core)
    right_band = pl.pallas_call(
        right_band_kernel,
        in_specs=[VMEM] * 2,
        out_specs=VMEM,
        out_shape=jax.ShapeDtypeStruct((9 * BLK, WIDE), BF16),
        compiler_params=params(16),
        cost_estimate=cost(0, 2 * MIB),
        name="right_band",
    )(halves, across)
    middle, total, to_chip, to_core, above_band = pl.pallas_call(
        first_right_kernel,
        in_specs=[VMEM] * 5 + [any_space] * 2 + [VMEM],
        out_specs=[VMEM] * 5,
        out_shape=[
            jax.ShapeDtypeStruct((2, TALL, WIDE), BF16),
            jax.ShapeDtypeStruct((2, TALL, WIDE), F32),
            jax.ShapeDtypeStruct((2, MARGIN, WIDE), BF16),
            jax.ShapeDtypeStruct((2, MARGIN, WIDE), BF16),
            jax.ShapeDtypeStruct((MARGIN, MARGIN), BF16),
        ],
        scratch_shapes=[pltpu.VMEM((2 * MARGIN + 2 * BLK, WIDE), BF16)] * 2 + [pltpu.SemaphoreType.DMA((2,))],
        compiler_params=params(20),
        cost_estimate=cost(4 * TALL * 9 * BLK * WIDE, 14 * MIB),
        name="first_right",
    )(before, density, after, left, right_band, from_chip, from_core, below_band)

    before = to_column(middle, 1)
    after = to_column(middle, -1)
    from_chip = to_other_chip(to_chip)
    from_core = to_other_core(to_core)
    total = pl.pallas_call(
        second_left_kernel,
        in_specs=[VMEM] * 4,
        out_specs=VMEM,
        out_shape=jax.ShapeDtypeStruct((2, TALL, WIDE), F32),
        compiler_params=params(24),
        cost_estimate=cost(2 * TALL * 1408 * 2 * WIDE, 10 * MIB),
        name="second_left",
    )(middle, left_band, right_band, total)
    return pl.pallas_call(
        last_kernel,
        in_specs=[VMEM] * 8,
        out_specs=any_space,
        out_shape=jax.ShapeDtypeStruct((2, TALL, WIDE), F32),
        scratch_shapes=[pltpu.VMEM((2, TALL, WIDE), F32), pltpu.SemaphoreType.DMA((4,))],
        compiler_params=params(16),
        cost_estimate=cost(4 * TALL * 6 * BLK * WIDE, 8 * MIB),
        name="last",
    )(before, after, total, right_band, from_chip, from_core, above_band, below_band)


def solution(mesh):
    placed = (P(None, "row", "col"), P("row", None), P("row", None, None, None))
    return jax.shard_map(
        on_device, mesh=mesh, in_specs=placed, out_specs=P(None, "row", "col"), check_vma=False
    )
```

```python
import functools

import jax
import jax.numpy as jnp
from jax import lax
from jax.experimental import pallas as pl
from jax.experimental.pallas import tpu as pltpu
from jax.sharding import PartitionSpec as P

BLK = 128
BAND = 3
DT = 0.5

Y_HI, X, CORE = 2, 4, 2
Y_LO, Z = 4, 8
ROWS = Y_HI * X * CORE
COLS = Y_LO * Z
TALL = 6 * BLK
WIDE = 3 * BLK
MARGIN = BAND * BLK
PAIR = 2 * BLK
HALF = TALL // 2

CROSSING = [(r, p) for r in range(-BAND, 0) for p in range(1, BAND + 1) if r + p >= 0]

F32 = jnp.float32
BF16 = jnp.bfloat16
MIB = 1 << 20
VMEM = pl.BlockSpec(memory_space=pltpu.VMEM)


def params(mib):
    return pltpu.CompilerParams(vmem_limit_bytes=mib * MIB)


def cost(flops, bytes_accessed):
    return pl.CostEstimate(flops=flops, bytes_accessed=bytes_accessed, transcendentals=0)


def to_column(block, distance):
    return lax.ppermute(block, "col", [(i - distance, i) for i in range(COLS) if 0 <= i - distance < COLS])


OWN_CHIPS = [
    0o57234610, 0o65324710, 0o47106532, 0o46217530, 0o75104623, 0o65314720, 0o47205631, 0o46107523, 0o41356207,
    0o61354207, 0o72046135, 0o42067135, 0o71354206, 0o41357206, 0o72064135, 0o76024135, 0o37516402, 0o17502463,
    0o24631750, 0o14602753, 0o37521460, 0o7632451, 0o14523760, 0o2735461, 0o64027513, 0o54217603, 0o76035421,
    0o75206413, 0o46137520, 0o75234601, 0o76015423, 0o65137420,
]
CROSSING_CHIPS = [
    0o46207531, 0o45107623, 0o67124530, 0o45126730, 0o65104732, 0o47325610, 0o57304612, 0o71045236, 0o50264731,
    0o60145732, 0o57324016, 0o62345017, 0o50176324, 0o72165034, 0o50246713, 0o23645017, 0o34721560, 0o54723601,
    0o36510472, 0o14520673, 0o56732401, 0o46032571, 0o17532640, 0o75136402, 0o45107623, 0o76034512, 0o46017523,
    0o76235401, 0o75106423, 0o56017423, 0o76235410,
]


def routes(kind, chips):
    pairs = []
    for tile in range(ROWS):
        for col in range(COLS):
            y_lo, z = divmod(col, Z)
            away = (z - 2 * tile + 1 - kind) % Z
            target = 2 * tile + away // 2 + kind
            if away < 4 and target < COLS:
                chip = chips[2 * tile + away // 2] >> 3 * (away % 2 * Y_LO + y_lo) & 7
                pairs.append((tile * COLS + col, (chip * CORE + kind) * COLS + target))
    return pairs


def core_index():
    return lax.rem(lax.axis_index("row"), CORE)


def start_kernel(hcols, hvals, upper, own, crossing, low):
    tile = lax.axis_index("row")
    z = lax.rem(lax.axis_index("col"), Z)
    for i in range(6):
        b = tile * 6 + i
        upper[4 * i] = hvals[i, 0]
        for p in range(1, BAND + 1):
            block = jnp.zeros((BLK, BLK), BF16)
            for s in range(1, p + 1):
                named = jnp.broadcast_to(hcols[s : s + 1, i : i + 1] == b + p, (BLK, BLK))
                block = jnp.where(named, hvals[i, s], block)
            upper[4 * i + p] = block
    away = lax.rem(z - 2 * tile + 1 + 2 * ROWS, Z)
    half = lax.rem(away // 2, 2)
    own[...] = upper[pl.ds(half * 12, 12)]
    away = lax.rem(z - 2 * tile + 2 * ROWS, Z)
    half = lax.rem(away // 2, 2)
    for k, (r, p) in enumerate(CROSSING):
        crossing[k] = upper[half * 12 + 4 * (r + 3) + p]
        low[k // 3 * BLK : (k // 3 + 1) * BLK, k % 3 * BLK : (k % 3 + 1) * BLK] = upper[4 * (r + 6) + p]


def edge(density, low, row):
    rows = lax.dynamic_slice_in_dim(density, row, MARGIN, 1)
    return jnp.concatenate([rows.reshape(2 * MARGIN, WIDE), low], axis=0)


def both(block):
    wide = block.astype(F32)
    return (wide + wide.T).astype(BF16)


def right_band_kernel(halves, across, band):
    core = core_index()

    def own(k):
        return jnp.where(core == 0, halves[k], across[k])

    def crossing(k):
        return jnp.where(core == 0, across[k], halves[k])

    for r in range(9):
        for j in range(3):
            offset = j + BAND - r
            if abs(offset) > BAND:
                block = jnp.zeros((BLK, BLK), BF16)
            elif offset > 0 and r < BAND:
                block = crossing(CROSSING.index((r - BAND, offset)))
            elif offset > 0:
                block = own(4 * (r - BAND) + offset)
            elif offset == 0:
                block = both(own(4 * j))
            else:
                block = own(4 * j - offset).T
            band[r * BLK : (r + 1) * BLK, j * BLK : (j + 1) * BLK] = block


def inner_products(band, field, pair):
    first, stop = max(0, pair * PAIR - MARGIN), min(TALL, pair * PAIR + PAIR + MARGIN)
    columns = slice(first - pair * PAIR + MARGIN, stop - pair * PAIR + MARGIN)
    both_parts = jnp.concatenate([field[0, first:stop], field[1, first:stop]], axis=1)
    return jnp.dot(band[pair][:, columns], both_parts, preferred_element_type=F32)


def first_left_kernel(field, upper, out, band, below_band):
    for pair in range(3):
        for i in range(2):
            b = 2 * pair + i
            for c in range(8):
                offset = c - BAND - i
                if abs(offset) > BAND or b + offset < 0:
                    block = jnp.zeros((BLK, BLK), BF16)
                elif offset > 0:
                    block = upper[4 * b + offset]
                elif offset == 0:
                    block = both(upper[4 * b])
                else:
                    block = upper[4 * (b + offset) - offset].T
                band[pair, i * BLK : (i + 1) * BLK, c * BLK : (c + 1) * BLK] = block
    for i in range(3):
        for c in range(3):
            block = upper[4 * (3 + i) + 3 + c - i] if c <= i else jnp.zeros((BLK, BLK), BF16)
            below_band[i * BLK : (i + 1) * BLK, c * BLK : (c + 1) * BLK] = block
    for pair in range(3):
        product = inner_products(band, field, pair)
        rows = slice(pair * PAIR, (pair + 1) * PAIR)
        out[0, rows] = product[:, :WIDE]
        out[1, rows] = product[:, WIDE:]


def first_right_kernel(
    before, field, after, left, band, chip_far, core_far, below_band,
    middle, total, to_chip, to_core, above_band, from_chip, from_core, sems,
):
    core = core_index()
    copies = [
        pltpu.make_async_copy(far, near, sems.at[k])
        for k, (far, near) in enumerate(((chip_far, from_chip), (core_far, from_core)))
    ]
    for copy in copies:
        copy.start()
    for part in range(2):
        for k in range(2):
            rows = slice(k * MARGIN, (k + 1) * MARGIN)
            stretch = jnp.concatenate([before[part, rows], field[part, rows], after[part, rows]], axis=1)
            product = jnp.concatenate(
                [
                    jnp.dot(stretch[:, :1024], band[:1024, :256], preferred_element_type=F32),
                    jnp.dot(stretch[:, 256:], band[256:, 256:], preferred_element_type=F32),
                ],
                axis=1,
            )
            total[1 - part, rows] = left[part, rows] - product
    for copy in copies:
        copy.wait()
    for i in range(3):
        for c in range(3):
            block = jnp.zeros((BLK, BLK), BF16)
            if c >= i:
                k = CROSSING.index((c - 3, i + 3 - c))
                rows = slice(2 * MARGIN + k // 3 * BLK, 2 * MARGIN + (k // 3 + 1) * BLK)
                at = slice(k % 3 * BLK, (k % 3 + 1) * BLK)
                block = jnp.where(core == 0, from_chip[rows, at], from_core[rows, at]).T
            above_band[i * BLK : (i + 1) * BLK, c * BLK : (c + 1) * BLK] = block
    for part in range(2):
        other, sign = 1 - part, (-1.0, 1.0)[part]
        one, two = (side[part * MARGIN : (part + 1) * MARGIN] for side in (from_chip, from_core))
        halves = (
            (above_band, jnp.where(core == 0, one, two)),
            (below_band, jnp.where(core == 0, two, one)),
        )
        for k, (outer, beyond) in enumerate(halves):
            rows = slice(k * MARGIN, (k + 1) * MARGIN)
            far = jnp.dot(outer[...], beyond, preferred_element_type=F32)
            rate = sign * (total[other, rows] + far)
            start = field[other, rows].astype(F32)
            middle[other, rows] = (start + DT * rate).astype(BF16)
            total[other, rows] = start + (DT / 2) * rate
        to_chip[other] = middle[other, pl.ds(pl.multiple_of(core * MARGIN, MARGIN), MARGIN)]
        to_core[other] = middle[other, pl.ds(pl.multiple_of((1 - core) * MARGIN, MARGIN), MARGIN)]


def second_left_kernel(middle, band, right_band, total, out):
    centre = right_band[MARGIN : MARGIN + WIDE, :]
    for pair in range(3):
        rows = slice(pair * PAIR, (pair + 1) * PAIR)
        product = inner_products(band, middle, pair)
        own_re = jnp.dot(middle[0, rows], centre, preferred_element_type=F32)
        own_im = jnp.dot(middle[1, rows], centre, preferred_element_type=F32)
        out[0, rows] = total[0, rows] + (DT / 2) * (product[:, WIDE:] - own_im)
        out[1, rows] = total[1, rows] - (DT / 2) * (product[:, :WIDE] - own_re)


def last_kernel(before, after, total, band, from_chip, from_core, above_band, below_band, out, result, sems):
    core = core_index()
    copies = []
    for part in range(2):
        other, sign = 1 - part, (-1.0, 1.0)[part]
        halves = (
            (above_band, jnp.where(core == 0, from_chip[part], from_core[part])),
            (below_band, jnp.where(core == 0, from_core[part], from_chip[part])),
        )
        for k, (outer, beyond) in enumerate(halves):
            rows = slice(k * MARGIN, (k + 1) * MARGIN)
            product = jnp.dot(before[part, rows], band[:MARGIN, :], preferred_element_type=F32)
            product = product + jnp.dot(after[part, rows], band[MARGIN + WIDE :, :], preferred_element_type=F32)
            far = jnp.dot(outer[...], beyond, preferred_element_type=F32)
            result[other, rows] = total[other, rows] + (sign * DT / 2) * (far - product)
            at = pl.ds(k * MARGIN, MARGIN)
            copies.append(pltpu.make_async_copy(result.at[other, at], out.at[other, at], sems.at[2 * part + k]))
            copies[-1].start()
    for copy in copies:
        copy.wait()


def to_other_core(block):
    return lax.ppermute(block, "row", [(i, i ^ 1) for i in range(ROWS)])


def to_other_chip(block):
    ends = [(i, i + 1) for i in range(1, ROWS - 1, 2)]
    return lax.ppermute(block, "row", ends + [(j, i) for i, j in ends])


def on_device(density, hcols, hvals):
    before = to_column(density, 1)
    after = to_column(density, -1)
    any_space = pl.BlockSpec(memory_space=pl.ANY)
    upper, own, crossing, low = pl.pallas_call(
        start_kernel,
        in_specs=[VMEM] * 2,
        out_specs=[VMEM] * 4,
        out_shape=[
            jax.ShapeDtypeStruct((24, BLK, BLK), BF16),
            jax.ShapeDtypeStruct((12, BLK, BLK), BF16),
            jax.ShapeDtypeStruct((6, BLK, BLK), BF16),
            jax.ShapeDtypeStruct((2 * BLK, WIDE), BF16),
        ],
        compiler_params=params(56),
        cost_estimate=cost(0, 2 * MIB),
        name="start",
    )(hcols.T, hvals)
    to_chip = edge(density, low, core_index() * MARGIN)
    to_core = edge(density, low, (1 - core_index()) * MARGIN)
    own = lax.ppermute(own, ("row", "col"), routes(0, OWN_CHIPS))
    crossing = lax.ppermute(crossing, ("row", "col"), routes(1, CROSSING_CHIPS))
    halves = jnp.where(core_index() == 0, own, jnp.concatenate([crossing, crossing], axis=0))
    across = to_other_core(halves)
    left, left_band, below_band = pl.pallas_call(
        first_left_kernel,
        in_specs=[VMEM] * 2,
        out_specs=[VMEM] * 3,
        out_shape=[
            jax.ShapeDtypeStruct((2, TALL, WIDE), F32),
            jax.ShapeDtypeStruct((3, PAIR, 1024), BF16),
            jax.ShapeDtypeStruct((MARGIN, MARGIN), BF16),
        ],
        compiler_params=params(20),
        cost_estimate=cost(2 * TALL * 1024 * 2 * WIDE, 8 * MIB),
        name="first_left",
    )(density, upper)
    to_core, _, _ = lax.optimization_barrier((to_core, crossing, left_band))
    from_chip = to_other_chip(to_chip)
    from_core = to_other_core(to_core)
    right_band = pl.pallas_call(
        right_band_kernel,
        in_specs=[VMEM] * 2,
        out_specs=VMEM,
        out_shape=jax.ShapeDtypeStruct((9 * BLK, WIDE), BF16),
        compiler_params=params(16),
        cost_estimate=cost(0, 2 * MIB),
        name="right_band",
    )(halves, across)
    middle, total, to_chip, to_core, above_band = pl.pallas_call(
        first_right_kernel,
        in_specs=[VMEM] * 5 + [any_space] * 2 + [VMEM],
        out_specs=[VMEM] * 5,
        out_shape=[
            jax.ShapeDtypeStruct((2, TALL, WIDE), BF16),
            jax.ShapeDtypeStruct((2, TALL, WIDE), F32),
            jax.ShapeDtypeStruct((2, MARGIN, WIDE), BF16),
            jax.ShapeDtypeStruct((2, MARGIN, WIDE), BF16),
            jax.ShapeDtypeStruct((MARGIN, MARGIN), BF16),
        ],
        scratch_shapes=[pltpu.VMEM((2 * MARGIN + 2 * BLK, WIDE), BF16)] * 2 + [pltpu.SemaphoreType.DMA((2,))],
        compiler_params=params(20),
        cost_estimate=cost(4 * TALL * 9 * BLK * WIDE, 14 * MIB),
        name="first_right",
    )(before, density, after, left, right_band, from_chip, from_core, below_band)

    before = to_column(middle, 1)
    after = to_column(middle, -1)
    from_chip = to_other_chip(to_chip)
    from_core = to_other_core(to_core)
    total = pl.pallas_call(
        second_left_kernel,
        in_specs=[VMEM] * 4,
        out_specs=VMEM,
        out_shape=jax.ShapeDtypeStruct((2, TALL, WIDE), F32),
        compiler_params=params(24),
        cost_estimate=cost(2 * TALL * 1408 * 2 * WIDE, 10 * MIB),
        name="second_left",
    )(middle, left_band, right_band, total)
    return pl.pallas_call(
        last_kernel,
        in_specs=[VMEM] * 8,
        out_specs=any_space,
        out_shape=jax.ShapeDtypeStruct((2, TALL, WIDE), F32),
        scratch_shapes=[pltpu.VMEM((2, TALL, WIDE), F32), pltpu.SemaphoreType.DMA((4,))],
        compiler_params=params(16),
        cost_estimate=cost(4 * TALL * 6 * BLK * WIDE, 8 * MIB),
        name="last",
    )(before, after, total, right_band, from_chip, from_core, above_band, below_band)


def solution(mesh):
    placed = (P(None, "row", "col"), P("row", None), P("row", None, None, None))
    return jax.shard_map(
        on_device, mesh=mesh, in_specs=placed, out_specs=P(None, "row", "col"), check_vma=False
    )
```

```python
import functools

import jax
import jax.numpy as jnp
from jax import lax
from jax.experimental import pallas as pl
from jax.experimental.pallas import tpu as pltpu
from jax.sharding import PartitionSpec as P

BLK = 128
BAND = 3
DT = 0.5

Y_HI, X, CORE = 2, 4, 2
Y_LO, Z = 4, 8
ROWS = Y_HI * X * CORE
COLS = Y_LO * Z
TALL = 6 * BLK
WIDE = 3 * BLK
MARGIN = BAND * BLK
PAIR = 2 * BLK
HALF = TALL // 2

CROSSING = [(r, p) for r in range(-BAND, 0) for p in range(1, BAND + 1) if r + p >= 0]

F32 = jnp.float32
BF16 = jnp.bfloat16
MIB = 1 << 20
VMEM = pl.BlockSpec(memory_space=pltpu.VMEM)


def params(mib):
    return pltpu.CompilerParams(vmem_limit_bytes=mib * MIB)


def cost(flops, bytes_accessed):
    return pl.CostEstimate(flops=flops, bytes_accessed=bytes_accessed, transcendentals=0)


def to_column(block, distance):
    return lax.ppermute(block, "col", [(i - distance, i) for i in range(COLS) if 0 <= i - distance < COLS])


OWN_CHIPS = [
    0o57234610, 0o65324710, 0o47106532, 0o46217530, 0o75104623, 0o65314720, 0o47205631, 0o46107523, 0o41356207,
    0o61354207, 0o72046135, 0o42067135, 0o71354206, 0o41357206, 0o72064135, 0o76024135, 0o37516402, 0o17502463,
    0o24631750, 0o14602753, 0o37521460, 0o7632451, 0o14523760, 0o2735461, 0o64027513, 0o54217603, 0o76035421,
    0o75206413, 0o46137520, 0o75234601, 0o76015423, 0o65137420,
]
CROSSING_CHIPS = [
    0o46207531, 0o45107623, 0o67124530, 0o45126730, 0o65104732, 0o47325610, 0o57304612, 0o71045236, 0o50264731,
    0o60145732, 0o57324016, 0o62345017, 0o50176324, 0o72165034, 0o50246713, 0o23645017, 0o34721560, 0o54723601,
    0o36510472, 0o14520673, 0o56732401, 0o46032571, 0o17532640, 0o75136402, 0o45107623, 0o76034512, 0o46017523,
    0o76235401, 0o75106423, 0o56017423, 0o76235410,
]


def routes(kind, chips):
    pairs = []
    for tile in range(ROWS):
        for col in range(COLS):
            y_lo, z = divmod(col, Z)
            away = (z - 2 * tile + 1 - kind) % Z
            target = 2 * tile + away // 2 + kind
            if away < 4 and target < COLS:
                chip = chips[2 * tile + away // 2] >> 3 * (away % 2 * Y_LO + y_lo) & 7
                pairs.append((tile * COLS + col, (chip * CORE + kind) * COLS + target))
    return pairs


def core_index():
    return lax.rem(lax.axis_index("row"), CORE)


def start_kernel(hcols, hvals, upper, own, crossing, low):
    tile = lax.axis_index("row")
    z = lax.rem(lax.axis_index("col"), Z)
    for i in range(6):
        b = tile * 6 + i
        upper[4 * i] = hvals[i, 0]
        for p in range(1, BAND + 1):
            block = jnp.zeros((BLK, BLK), BF16)
            for s in range(1, p + 1):
                named = jnp.broadcast_to(hcols[s : s + 1, i : i + 1] == b + p, (BLK, BLK))
                block = jnp.where(named, hvals[i, s], block)
            upper[4 * i + p] = block
    away = lax.rem(z - 2 * tile + 1 + 2 * ROWS, Z)
    half = lax.rem(away // 2, 2)
    own[...] = upper[pl.ds(half * 12, 12)]
    away = lax.rem(z - 2 * tile + 2 * ROWS, Z)
    half = lax.rem(away // 2, 2)
    for k, (r, p) in enumerate(CROSSING):
        crossing[k] = upper[half * 12 + 4 * (r + 3) + p]
        low[k // 3 * BLK : (k // 3 + 1) * BLK, k % 3 * BLK : (k % 3 + 1) * BLK] = upper[4 * (r + 6) + p]


def edge(density, low, row):
    rows = lax.dynamic_slice_in_dim(density, row, MARGIN, 1)
    return jnp.concatenate([rows.reshape(2 * MARGIN, WIDE), low], axis=0)


def both(block):
    wide = block.astype(F32)
    return (wide + wide.T).astype(BF16)


def right_band_kernel(halves, across, band):
    core = core_index()

    def own(k):
        return jnp.where(core == 0, halves[k], across[k])

    def crossing(k):
        return jnp.where(core == 0, across[k], halves[k])

    for r in range(9):
        for j in range(3):
            offset = j + BAND - r
            if abs(offset) > BAND:
                block = jnp.zeros((BLK, BLK), BF16)
            elif offset > 0 and r < BAND:
                block = crossing(CROSSING.index((r - BAND, offset)))
            elif offset > 0:
                block = own(4 * (r - BAND) + offset)
            elif offset == 0:
                block = both(own(4 * j))
            else:
                block = own(4 * j - offset).T
            band[r * BLK : (r + 1) * BLK, j * BLK : (j + 1) * BLK] = block


def inner_products(band, field, pair):
    first, stop = max(0, pair * PAIR - MARGIN), min(TALL, pair * PAIR + PAIR + MARGIN)
    columns = slice(first - pair * PAIR + MARGIN, stop - pair * PAIR + MARGIN)
    both_parts = jnp.concatenate([field[0, first:stop], field[1, first:stop]], axis=1)
    return jnp.dot(band[pair][:, columns], both_parts, preferred_element_type=F32)


def first_left_kernel(field, upper, out, band, below_band):
    for pair in range(3):
        for i in range(2):
            b = 2 * pair + i
            for c in range(8):
                offset = c - BAND - i
                if abs(offset) > BAND or b + offset < 0:
                    block = jnp.zeros((BLK, BLK), BF16)
                elif offset > 0:
                    block = upper[4 * b + offset]
                elif offset == 0:
                    block = both(upper[4 * b])
                else:
                    block = upper[4 * (b + offset) - offset].T
                band[pair, i * BLK : (i + 1) * BLK, c * BLK : (c + 1) * BLK] = block
    for i in range(3):
        for c in range(3):
            block = upper[4 * (3 + i) + 3 + c - i] if c <= i else jnp.zeros((BLK, BLK), BF16)
            below_band[i * BLK : (i + 1) * BLK, c * BLK : (c + 1) * BLK] = block
    for pair in range(3):
        product = inner_products(band, field, pair)
        rows = slice(pair * PAIR, (pair + 1) * PAIR)
        out[0, rows] = product[:, :WIDE]
        out[1, rows] = product[:, WIDE:]


def first_right_kernel(
    before, field, after, left, band, from_chip, from_core, below_band,
    middle, total, to_chip, to_core, above_band,
):
    core = core_index()
    for i in range(3):
        for c in range(3):
            block = jnp.zeros((BLK, BLK), BF16)
            if c >= i:
                k = CROSSING.index((c - 3, i + 3 - c))
                rows = slice(2 * MARGIN + k // 3 * BLK, 2 * MARGIN + (k // 3 + 1) * BLK)
                at = slice(k % 3 * BLK, (k % 3 + 1) * BLK)
                block = jnp.where(core == 0, from_chip[rows, at], from_core[rows, at]).T
            above_band[i * BLK : (i + 1) * BLK, c * BLK : (c + 1) * BLK] = block
    for part in range(2):
        other, sign = 1 - part, (-1.0, 1.0)[part]
        one, two = (side[part * MARGIN : (part + 1) * MARGIN] for side in (from_chip, from_core))
        halves = (
            (above_band, jnp.where(core == 0, one, two)),
            (below_band, jnp.where(core == 0, two, one)),
        )
        for k, (outer, beyond) in enumerate(halves):
            rows = slice(k * MARGIN, (k + 1) * MARGIN)
            stretch = jnp.concatenate([before[part, rows], field[part, rows], after[part, rows]], axis=1)
            product = jnp.concatenate(
                [
                    jnp.dot(stretch[:, :1024], band[:1024, :256], preferred_element_type=F32),
                    jnp.dot(stretch[:, 256:], band[256:, 256:], preferred_element_type=F32),
                ],
                axis=1,
            )
            far = jnp.dot(outer[...], beyond, preferred_element_type=F32)
            rate = sign * (left[part, rows] + far - product)
            start = field[other, rows].astype(F32)
            middle[other, rows] = (start + DT * rate).astype(BF16)
            total[other, rows] = start + (DT / 2) * rate
        to_chip[other] = middle[other, pl.ds(pl.multiple_of(core * MARGIN, MARGIN), MARGIN)]
        to_core[other] = middle[other, pl.ds(pl.multiple_of((1 - core) * MARGIN, MARGIN), MARGIN)]


def second_left_kernel(middle, band, right_band, total, out):
    centre = right_band[MARGIN : MARGIN + WIDE, :]
    for pair in range(3):
        rows = slice(pair * PAIR, (pair + 1) * PAIR)
        product = inner_products(band, middle, pair)
        own_re = jnp.dot(middle[0, rows], centre, preferred_element_type=F32)
        own_im = jnp.dot(middle[1, rows], centre, preferred_element_type=F32)
        out[0, rows] = total[0, rows] + (DT / 2) * (product[:, WIDE:] - own_im)
        out[1, rows] = total[1, rows] - (DT / 2) * (product[:, :WIDE] - own_re)


def last_kernel(before, after, total, band, from_chip, from_core, above_band, below_band, out, result, sems):
    core = core_index()
    copies = []
    for part in range(2):
        other, sign = 1 - part, (-1.0, 1.0)[part]
        halves = (
            (above_band, jnp.where(core == 0, from_chip[part], from_core[part])),
            (below_band, jnp.where(core == 0, from_core[part], from_chip[part])),
        )
        for k, (outer, beyond) in enumerate(halves):
            rows = slice(k * MARGIN, (k + 1) * MARGIN)
            product = jnp.dot(before[part, rows], band[:MARGIN, :], preferred_element_type=F32)
            product = product + jnp.dot(after[part, rows], band[MARGIN + WIDE :, :], preferred_element_type=F32)
            far = jnp.dot(outer[...], beyond, preferred_element_type=F32)
            result[other, rows] = total[other, rows] + (sign * DT / 2) * (far - product)
            at = pl.ds(k * MARGIN, MARGIN)
            copies.append(pltpu.make_async_copy(result.at[other, at], out.at[other, at], sems.at[2 * part + k]))
            copies[-1].start()
    for copy in copies:
        copy.wait()


def to_other_core(block):
    return lax.ppermute(block, "row", [(i, i ^ 1) for i in range(ROWS)])


def to_other_chip(block):
    ends = [(i, i + 1) for i in range(1, ROWS - 1, 2)]
    return lax.ppermute(block, "row", ends + [(j, i) for i, j in ends])


def on_device(density, hcols, hvals):
    before = to_column(density, 1)
    after = to_column(density, -1)
    any_space = pl.BlockSpec(memory_space=pl.ANY)
    upper, own, crossing, low = pl.pallas_call(
        start_kernel,
        in_specs=[VMEM] * 2,
        out_specs=[VMEM] * 4,
        out_shape=[
            jax.ShapeDtypeStruct((24, BLK, BLK), BF16),
            jax.ShapeDtypeStruct((12, BLK, BLK), BF16),
            jax.ShapeDtypeStruct((6, BLK, BLK), BF16),
            jax.ShapeDtypeStruct((2 * BLK, WIDE), BF16),
        ],
        compiler_params=params(56),
        cost_estimate=cost(0, 2 * MIB),
        name="start",
    )(hcols.T, hvals)
    to_chip = edge(density, low, core_index() * MARGIN)
    to_core = edge(density, low, (1 - core_index()) * MARGIN)
    own = lax.ppermute(own, ("row", "col"), routes(0, OWN_CHIPS))
    crossing = lax.ppermute(crossing, ("row", "col"), routes(1, CROSSING_CHIPS))
    left, left_band, below_band = pl.pallas_call(
        first_left_kernel,
        in_specs=[VMEM] * 2,
        out_specs=[VMEM] * 3,
        out_shape=[
            jax.ShapeDtypeStruct((2, TALL, WIDE), F32),
            jax.ShapeDtypeStruct((3, PAIR, 1024), BF16),
            jax.ShapeDtypeStruct((MARGIN, MARGIN), BF16),
        ],
        compiler_params=params(20),
        cost_estimate=cost(2 * TALL * 1024 * 2 * WIDE, 8 * MIB),
        name="first_left",
    )(density, upper)
    own, _ = lax.optimization_barrier((own, left_band))
    halves = jnp.where(core_index() == 0, own, jnp.concatenate([crossing, crossing], axis=0))
    across = to_other_core(halves)
    to_core, _ = lax.optimization_barrier((to_core, crossing))
    from_chip = to_other_chip(to_chip)
    from_core = to_other_core(to_core)
    right_band = pl.pallas_call(
        right_band_kernel,
        in_specs=[VMEM] * 2,
        out_specs=VMEM,
        out_shape=jax.ShapeDtypeStruct((9 * BLK, WIDE), BF16),
        compiler_params=params(16),
        cost_estimate=cost(0, 2 * MIB),
        name="right_band",
    )(halves, across)
    middle, total, to_chip, to_core, above_band = pl.pallas_call(
        first_right_kernel,
        in_specs=[VMEM] * 8,
        out_specs=[VMEM] * 5,
        out_shape=[
            jax.ShapeDtypeStruct((2, TALL, WIDE), BF16),
            jax.ShapeDtypeStruct((2, TALL, WIDE), F32),
            jax.ShapeDtypeStruct((2, MARGIN, WIDE), BF16),
            jax.ShapeDtypeStruct((2, MARGIN, WIDE), BF16),
            jax.ShapeDtypeStruct((MARGIN, MARGIN), BF16),
        ],
        compiler_params=params(20),
        cost_estimate=cost(4 * TALL * 9 * BLK * WIDE, 14 * MIB),
        name="first_right",
    )(before, density, after, left, right_band, from_chip, from_core, below_band)

    before = to_column(middle, 1)
    after = to_column(middle, -1)
    from_chip = to_other_chip(to_chip)
    from_core = to_other_core(to_core)
    total = pl.pallas_call(
        second_left_kernel,
        in_specs=[VMEM] * 4,
        out_specs=VMEM,
        out_shape=jax.ShapeDtypeStruct((2, TALL, WIDE), F32),
        compiler_params=params(24),
        cost_estimate=cost(2 * TALL * 1408 * 2 * WIDE, 10 * MIB),
        name="second_left",
    )(middle, left_band, right_band, total)
    return pl.pallas_call(
        last_kernel,
        in_specs=[VMEM] * 8,
        out_specs=any_space,
        out_shape=jax.ShapeDtypeStruct((2, TALL, WIDE), F32),
        scratch_shapes=[pltpu.VMEM((2, TALL, WIDE), F32), pltpu.SemaphoreType.DMA((4,))],
        compiler_params=params(16),
        cost_estimate=cost(4 * TALL * 6 * BLK * WIDE, 8 * MIB),
        name="last",
    )(before, after, total, right_band, from_chip, from_core, above_band, below_band)


def solution(mesh):
    placed = (P(None, "row", "col"), P("row", None), P("row", None, None, None))
    return jax.shard_map(
        on_device, mesh=mesh, in_specs=placed, out_specs=P(None, "row", "col"), check_vma=False
    )
```
